128 devices in a mesh: row: 32 (over y, x, core), col: 4 (over z).
Axes of the slice: x: 4, y: 4, z: 4, core: 2. Of those that a mesh axis runs over, the one named last changes fastest.
Arguments:
- layer_input: bfloat16 [1024, 6144], P('row', 'col'), may hold values from -6 to 6
- out_cotangent: bfloat16 [1024, 6144], P('row', 'col'), may hold values from -6 to 6
- preact: bfloat16 [1024, 49152], P('col', 'row'), may hold values from -8 to 8
- up_weight: bfloat16 [6144, 49152], P('col', 'row'), may hold values from -0.078125 to 0.078125
- down_weight: bfloat16 [49152, 6144], P('row', 'col'), may hold values from -0.02734375 to 0.02734375
Outputs:
- input_grad: bfloat16 [1024, 6144], P('row', 'col')
- up_grad: bfloat16 [6144, 49152], P('col', 'row')
- down_grad: bfloat16 [49152, 6144], P('row', 'col')
The draws below stay inside these ranges and needn't reach their ends.
All inputs are finite; a program needn't handle non-finite values.
Results may differ from the reference program's by a relative error of at most 0.02.
Values may be sent and summed in bfloat16 or wider, within the bound.
No kernel may reach another device: no remote copies, remote signals or barrier semaphores. Data moves between devices by JAX's collectives and lax.ppermute only.
A program may use at most 128 MiB of HBM per device.

```python
import math
import jax
import jax.numpy as jnp

D = 6144
F = 49152
TOKENS = 1024


def shard_levels(rng, shape, split, least, high):
    gain, own = 1.0, jax.random.fold_in(rng, 6)
    for position, blocks in split:
        steps = jnp.exp(jax.random.uniform(jax.random.fold_in(own, position), (blocks,), jnp.float32, least / len(split), high / len(split)))
        gain = gain * jnp.repeat(steps, shape[position] // blocks).reshape([-1 if axis == position else 1 for axis in range(len(shape))])
    return gain


def bell_draw(own_key, dims, width, bound, cuts=(), kind=jnp.bfloat16):
    level = shard_levels(own_key, dims, cuts, -0.22, 0.18) if cuts else 1.0
    result = jax.random.normal(own_key, dims, jnp.float32) * width * level
    return jnp.minimum(jnp.maximum(result, -bound), bound).astype(kind)


def setup_inputs(seed: int = 0) -> dict:
    streams_of = jax.random.split(jax.random.key(seed), 6)
    return {
        "layer_input": bell_draw(streams_of[0], (TOKENS, D), 1.0, 6.0, ((0, 32), (1, 4))),
        "out_cotangent": bell_draw(streams_of[1], (TOKENS, D), 1.0, 6.0, ((0, 32), (1, 4))),
        "preact": bell_draw(streams_of[2], (TOKENS, F), 1.5, 8.0, ((0, 4), (1, 32))),
        "up_weight": bell_draw(streams_of[3], (D, F), D ** -0.5, 0.078125, ((0, 4), (1, 32))),
        "down_weight": bell_draw(streams_of[4], (F, D), F ** -0.5, 0.02734375, ((0, 32), (1, 4))),
    }


def gelu_parts(pre):
    coeff = math.sqrt(2.0 / math.pi)
    inner = coeff * (pre + 0.044715 * pre * pre * pre)
    tangent = jnp.tanh(inner)
    activated = 0.5 * pre * (1.0 + tangent)
    slope = 0.5 * (1.0 + tangent) + 0.5 * pre * (1.0 - tangent * tangent) * coeff * (1.0 + 3.0 * 0.044715 * pre * pre)
    return (activated, slope)

def reference(layer_input, out_cotangent, preact, up_weight, down_weight):
    activated, slope = gelu_parts(preact.astype(jnp.float32))
    activated = activated.astype(jnp.bfloat16)
    act_grad = jnp.dot(out_cotangent, down_weight.T, preferred_element_type=jnp.float32)
    hidden_grad = (act_grad * slope).astype(jnp.bfloat16)
    down_grad = jnp.dot(activated.T, out_cotangent, preferred_element_type=jnp.float32).astype(jnp.bfloat16)
    up_grad = jnp.dot(layer_input.T, hidden_grad, preferred_element_type=jnp.float32).astype(jnp.bfloat16)
    input_grad = jnp.dot(hidden_grad, up_weight.T, preferred_element_type=jnp.float32).astype(jnp.bfloat16)
    return (input_grad, up_grad, down_grad)
```

```python
import math

import jax
import jax.numpy as jnp
from jax import lax
from jax.sharding import PartitionSpec as P

BF16 = jnp.bfloat16
F32 = jnp.float32
NY, NX, NZ = 4, 4, 4
CHUNKS = 2
SHIFTS = (1, -1, 2)


def device(y, x, core):
    return ((y % NY) * NX + x % NX) * 2 + core


def places():
    return [(y, x, core) for y in range(NY) for x in range(NX) for core in range(2)]


SIBLING = [(device(y, x, c), device(y, x, 1 - c)) for y, x, c in places()]


def plane_step(shift, x_core):
    return [
        (device(y, x, c), device(y, x + shift, c) if c == x_core else device(y + shift, x, c))
        for y, x, c in places()
    ]


def z_step(shift):
    return [(z, (z + shift) % NZ) for z in range(NZ)]


Z_BY_CORE = [
    (device(y, x, c) * NZ + z, device(y, x, c) * NZ + (z + (1 if c == 0 else -1)) % NZ)
    for y, x, c in places()
    for z in range(NZ)
]


def swap_cores(v):
    return lax.ppermute(v, "row", SIBLING)


def send_z(v, shift):
    return lax.ppermute(v, "col", z_step(shift))


def send_z_by_core(v):
    return lax.ppermute(v, ("row", "col"), Z_BY_CORE)


def dot(a, b, ca, cb):
    return lax.dot_general(a, b, (((ca,), (cb,)), ((), ())), preferred_element_type=F32)


def put(buf, piece, index):
    start = (index % buf.shape[0],) + (0,) * (buf.ndim - 1)
    return lax.dynamic_update_slice(buf, piece[None], start)


def take(buf, index):
    return lax.dynamic_index_in_dim(buf, index % buf.shape[0], 0, keepdims=False)


def gelu_parts(pre):
    coeff = math.sqrt(2.0 / math.pi)
    tangent = jnp.tanh(coeff * (pre + 0.044715 * pre * pre * pre))
    activated = 0.5 * pre * (1.0 + tangent)
    slope = 0.5 * (1.0 + tangent) + 0.5 * pre * (1.0 - tangent * tangent) * coeff * (
        1.0 + 3.0 * 0.044715 * pre * pre
    )
    return (activated, slope)


def after(v, *done):
    return lax.optimization_barrier((v,) + done)[0]


def ordered(even, ours, other, axis):
    return jnp.where(
        even, jnp.concatenate([ours, other], axis), jnp.concatenate([other, ours], axis)
    )


def halves(v, even):
    n = v.shape[-1] // 2
    left, right = v[..., :n], v[..., n:]
    return jnp.where(even, left, right), jnp.where(even, right, left)


def line_send(v, x_core):
    return [lax.ppermute(v, "row", plane_step(shift, x_core)) for shift in SHIFTS]


def line_join(v, pieces, place):
    out = put(jnp.zeros((4,) + v.shape, v.dtype), v, place)
    for shift, piece in zip(SHIFTS, pieces):
        out = put(out, piece, place - shift)
    return out


def line_reduce(v, place, x_core):
    pieces = [
        lax.ppermute(take(v, place + shift), "row", plane_step(shift, x_core)) for shift in SHIFTS
    ]
    total = take(v, place).astype(F32)
    for piece in pieces:
        total = total + piece.astype(F32)
    return total


def local(layer_input, out_cotangent, preact, up_weight, down_weight):
    row, z = lax.axis_index("row"), lax.axis_index("col")
    even, x, y = row % 2 == 0, (row // 2) % NX, row // (2 * NX)
    first, second = jnp.where(even, x, y), jnp.where(even, y, x)

    ours, theirs = halves(jnp.stack([out_cotangent, layer_input]), even)
    pair = ordered(even, ours, swap_cores(theirs), 1)
    pieces = line_send(pair, 0)
    cot_line = line_join(pair[0], [p[0] for p in pieces], first)
    input_line = line_join(pair[1], [p[1] for p in pieces], first)

    activated, slope = gelu_parts(after(preact, pair).astype(F32))
    activated = activated.astype(BF16)
    act_below, act_above = send_z(activated, 1), send_z(activated, -1)

    pieces = line_send(cot_line, 1)
    cot = line_join(cot_line, pieces, second)
    cot = jnp.where(even, cot, cot.swapaxes(0, 1)).reshape(-1, cot.shape[-1])
    cot = ordered(even, cot, swap_cores(cot), 1)
    tokens = cot.reshape(NZ, -1, cot.shape[1])
    slope = after(slope, cot_line)

    pieces = line_send(after(input_line, cot), 1)
    inputs = line_join(input_line, pieces, second)
    inputs = jnp.where(even, inputs, inputs.swapaxes(0, 1)).reshape(-1, inputs.shape[-1])
    inputs = ordered(even, inputs, swap_cores(inputs), 1)

    width = down_weight.shape[0] // CHUNKS

    def share(k, shift):
        return dot(take(tokens, z + shift), down_weight[k * width : (k + 1) * width], 1, 1)

    chunks = range(CHUNKS)
    far = [send_z_by_core(share(k, 2).astype(BF16)) for k in chunks]
    act_far = send_z_by_core(jnp.where(even, act_below, act_above))

    sides = []
    for k in chunks:
        got = far[k].astype(F32)
        zero = jnp.zeros_like(got)
        up = (share(k, 1) + jnp.where(even, got, zero)).astype(BF16)
        down = (share(k, -1) + jnp.where(even, zero, got)).astype(BF16)
        sides.append((send_z(up, 1), send_z(down, -1)))
    own, near = [], []
    for k in chunks:
        total = share(k, 0) + sides[k][0].astype(F32) + sides[k][1].astype(F32)
        own.append((total * slope[:, k * width : (k + 1) * width]).astype(BF16))
        near.append((send_z(own[k], 1), send_z(own[k], -1)))

    act_all = jnp.zeros((NZ,) + activated.shape, BF16)
    for shift, block in ((0, activated), (-1, act_below), (1, act_above), (2, act_far)):
        act_all = put(act_all, block, z + shift)
    down_grad = dot(act_all.reshape(-1, act_all.shape[2]), cot, 0, 0).astype(BF16)

    last = []
    for k in chunks:
        onward = jnp.where(even, *near[k])
        if k == 0:
            onward = after(onward, down_grad)
        last.append(send_z_by_core(onward))

    hidden = jnp.zeros((NZ,) + preact.shape, BF16)
    plane = jnp.zeros((NY,) + (preact.shape[0], up_weight.shape[0] // 2), BF16)
    for shift, blocks in (
        (0, own),
        (-1, [n[0] for n in near]),
        (1, [n[1] for n in near]),
        (2, last),
    ):
        block = jnp.concatenate(blocks, axis=1)
        hidden = put(hidden, block, z + shift)
        ours, theirs = halves(dot(block, up_weight, 1, 1).astype(BF16), even)
        plane = put(plane, (ours + swap_cores(theirs).astype(F32)).astype(BF16), z + shift)

    plane = plane.reshape(NY, NX, -1, plane.shape[-1])
    line = line_reduce(jnp.where(even, plane, plane.swapaxes(0, 1)), second, 1).astype(BF16)
    up_grad = dot(inputs, hidden.reshape(-1, hidden.shape[2]), 0, 0).astype(BF16)
    pair = line_reduce(after(line, up_grad), first, 0).astype(BF16)
    n = pair.shape[0] // 2
    upper, lower = pair[:n], pair[n:]
    other = swap_cores(jnp.where(even, lower, upper))
    input_grad = ordered(even, jnp.where(even, upper, lower), other, 1)
    return (input_grad, up_grad, down_grad)


def solution(mesh):
    in_specs = (P("row", "col"), P("row", "col"), P("col", "row"), P("col", "row"), P("row", "col"))
    out_specs = (P("row", "col"), P("col", "row"), P("row", "col"))
    return jax.shard_map(local, mesh=mesh, in_specs=in_specs, out_specs=out_specs, check_vma=False)
```

```python
import math

import jax
import jax.numpy as jnp
from jax import lax
from jax.sharding import PartitionSpec as P

BF16 = jnp.bfloat16
F32 = jnp.float32
NY, NX, NZ = 4, 4, 4
CHUNKS = 2
SHIFTS = (1, -1, 2)


def device(y, x, core):
    return ((y % NY) * NX + x % NX) * 2 + core


def places():
    return [(y, x, core) for y in range(NY) for x in range(NX) for core in range(2)]


SIBLING = [(device(y, x, c), device(y, x, 1 - c)) for y, x, c in places()]


def plane_step(shift, x_core):
    return [
        (device(y, x, c), device(y, x + shift, c) if c == x_core else device(y + shift, x, c))
        for y, x, c in places()
    ]


def z_step(shift):
    return [(z, (z + shift) % NZ) for z in range(NZ)]


Z_BY_CORE = [
    (device(y, x, c) * NZ + z, device(y, x, c) * NZ + (z + (1 if c == 0 else -1)) % NZ)
    for y, x, c in places()
    for z in range(NZ)
]


def swap_cores(v):
    return lax.ppermute(v, "row", SIBLING)


def send_z(v, shift):
    return lax.ppermute(v, "col", z_step(shift))


def send_z_by_core(v):
    return lax.ppermute(v, ("row", "col"), Z_BY_CORE)


def dot(a, b, ca, cb):
    return lax.dot_general(a, b, (((ca,), (cb,)), ((), ())), preferred_element_type=F32)


def put(buf, piece, index):
    start = (index % buf.shape[0],) + (0,) * (buf.ndim - 1)
    return lax.dynamic_update_slice(buf, piece[None], start)


def take(buf, index):
    return lax.dynamic_index_in_dim(buf, index % buf.shape[0], 0, keepdims=False)


def gelu_parts(pre):
    coeff = math.sqrt(2.0 / math.pi)
    tangent = jnp.tanh(coeff * (pre + 0.044715 * pre * pre * pre))
    activated = 0.5 * pre * (1.0 + tangent)
    slope = 0.5 * (1.0 + tangent) + 0.5 * pre * (1.0 - tangent * tangent) * coeff * (
        1.0 + 3.0 * 0.044715 * pre * pre
    )
    return (activated, slope)


def after(v, *done):
    return lax.optimization_barrier((v, done))[0]


def ordered(even, ours, other, axis):
    return jnp.where(
        even, jnp.concatenate([ours, other], axis), jnp.concatenate([other, ours], axis)
    )


def halves(v, even):
    n = v.shape[-1] // 2
    left, right = v[..., :n], v[..., n:]
    return jnp.where(even, left, right), jnp.where(even, right, left)


def line_send(v, x_core):
    return [lax.ppermute(v, "row", plane_step(shift, x_core)) for shift in SHIFTS]


def line_join(v, pieces, place):
    out = put(jnp.zeros((4,) + v.shape, v.dtype), v, place)
    for shift, piece in zip(SHIFTS, pieces):
        out = put(out, piece, place - shift)
    return out


def line_reduce(v, place, x_core, *done):
    pieces = [
        lax.ppermute(take(v, place + shift), "row", plane_step(shift, x_core)) for shift in SHIFTS
    ]
    total = take(v, place).astype(F32)
    for piece in after(pieces, *done):
        total = total + piece.astype(F32)
    return total


def local(layer_input, out_cotangent, preact, up_weight, down_weight):
    row, z = lax.axis_index("row"), lax.axis_index("col")
    even, x, y = row % 2 == 0, (row // 2) % NX, row // (2 * NX)
    first, second = jnp.where(even, x, y), jnp.where(even, y, x)

    ours, theirs = halves(jnp.stack([out_cotangent, layer_input]), even)
    pair = ordered(even, ours, swap_cores(theirs), 1)
    pieces = line_send(pair, 0)
    cot_line = line_join(pair[0], [p[0] for p in pieces], first)
    input_line = line_join(pair[1], [p[1] for p in pieces], first)

    activated, slope = gelu_parts(after(preact, pair).astype(F32))
    activated = activated.astype(BF16)
    act_below, act_above = send_z(activated, 1), send_z(activated, -1)

    pieces = line_send(cot_line, 1)
    cot = line_join(cot_line, pieces, second)
    cot = jnp.where(even, cot, cot.swapaxes(0, 1)).reshape(-1, cot.shape[-1])
    cot = ordered(even, cot, swap_cores(cot), 1)
    cot = after(cot, act_below, act_above)
    tokens = cot.reshape(NZ, -1, cot.shape[1])
    slope = after(slope, cot_line)

    width = down_weight.shape[0] // CHUNKS
    chunks = range(CHUNKS)

    def share(k, shift):
        return dot(take(tokens, z + shift), down_weight[k * width : (k + 1) * width], 1, 1)

    opposite = [share(k, 2).astype(BF16) for k in chunks]
    far = [send_z_by_core(v) for v in opposite]
    sides = []
    for k in chunks:
        got = far[k].astype(F32)
        zero = jnp.zeros_like(got)
        up = (share(k, 1) + jnp.where(even, got, zero)).astype(BF16)
        down = (share(k, -1) + jnp.where(even, zero, got)).astype(BF16)
        sides.append([send_z(up, 1), send_z(down, -1)])

    own, near = [], []
    for k in chunks:
        if k > 0:
            sides[k] = after(sides[k], own[k - 1])
        total = share(k, 0) + sides[k][0].astype(F32) + sides[k][1].astype(F32)
        own.append((total * slope[:, k * width : (k + 1) * width]).astype(BF16))
        near.append([send_z(own[k], 1), send_z(own[k], -1)])

    input_pieces = line_send(after(input_line, own[-1]), 1)


    last = []
    for k in chunks:
        if k > 0:
            near[k] = after(near[k], onward)
        onward = jnp.where(even, *near[k])
        last.append(send_z_by_core(onward))

    act_far = send_z_by_core(after(jnp.where(even, act_below, act_above), onward))
    act_all = jnp.zeros((NZ,) + activated.shape, BF16)
    for shift, block in ((0, activated), (-1, act_below), (1, act_above), (2, act_far)):
        act_all = put(act_all, block, z + shift)
    down_grad = dot(act_all.reshape(-1, act_all.shape[2]), cot, 0, 0).astype(BF16)

    last[-1] = after(last[-1], input_pieces)
    inputs = line_join(input_line, input_pieces, second)
    inputs = jnp.where(even, inputs, inputs.swapaxes(0, 1)).reshape(-1, inputs.shape[-1])
    inputs = ordered(even, inputs, swap_cores(inputs), 1)

    hidden = jnp.zeros((NZ,) + preact.shape, BF16)
    plane = jnp.zeros((NY,) + (preact.shape[0], up_weight.shape[0] // 2), BF16)
    for shift, blocks in (
        (0, own),
        (-1, [n[0] for n in near]),
        (1, [n[1] for n in near]),
        (2, last),
    ):
        block = jnp.concatenate(blocks, axis=1)
        hidden = put(hidden, block, z + shift)
        ours, theirs = halves(dot(block, up_weight, 1, 1).astype(BF16), even)
        plane = put(plane, (ours + swap_cores(theirs).astype(F32)).astype(BF16), z + shift)
    up_grad = dot(inputs, hidden.reshape(-1, hidden.shape[2]), 0, 0).astype(BF16)

    plane = plane.reshape(NY, NX, -1, plane.shape[-1])
    plane = jnp.where(even, plane, plane.swapaxes(0, 1))
    line = line_reduce(plane, second, 1, up_grad).astype(BF16)
    pair = line_reduce(line, first, 0).astype(BF16)
    n = pair.shape[0] // 2
    upper, lower = pair[:n], pair[n:]
    other = swap_cores(jnp.where(even, lower, upper))
    input_grad = ordered(even, jnp.where(even, upper, lower), other, 1)
    return (input_grad, up_grad, down_grad)


def solution(mesh):
    in_specs = (P("row", "col"), P("row", "col"), P("col", "row"), P("col", "row"), P("row", "col"))
    out_specs = (P("row", "col"), P("col", "row"), P("row", "col"))
    return jax.shard_map(local, mesh=mesh, in_specs=in_specs, out_specs=out_specs, check_vma=False)
```

```python
import math

import jax
import jax.numpy as jnp
from jax import lax
from jax.sharding import PartitionSpec as P

BF16 = jnp.bfloat16
F32 = jnp.float32
NY, NX, NZ = 4, 4, 4
CHUNKS = 2
SHIFTS = (2, 1, -1)


def device(y, x, core):
    return ((y % NY) * NX + x % NX) * 2 + core


def places():
    return [(y, x, core) for y in range(NY) for x in range(NX) for core in range(2)]


SIBLING = [(device(y, x, c), device(y, x, 1 - c)) for y, x, c in places()]


def plane_step(shift, x_core):
    return [
        (device(y, x, c), device(y, x + shift, c) if c == x_core else device(y + shift, x, c))
        for y, x, c in places()
    ]


def z_step(shift):
    return [(z, (z + shift) % NZ) for z in range(NZ)]


Z_BY_CORE = [
    (device(y, x, c) * NZ + z, device(y, x, c) * NZ + (z + (1 if c == 0 else -1)) % NZ)
    for y, x, c in places()
    for z in range(NZ)
]


def swap_cores(v):
    return lax.ppermute(v, "row", SIBLING)


def send_z(v, shift):
    return lax.ppermute(v, "col", z_step(shift))


def send_z_by_core(v):
    return lax.ppermute(v, ("row", "col"), Z_BY_CORE)


def dot(a, b, ca, cb):
    return lax.dot_general(a, b, (((ca,), (cb,)), ((), ())), preferred_element_type=F32)


def put(buf, piece, index):
    start = (index % buf.shape[0],) + (0,) * (buf.ndim - 1)
    return lax.dynamic_update_slice(buf, piece[None], start)


def take(buf, index):
    return lax.dynamic_index_in_dim(buf, index % buf.shape[0], 0, keepdims=False)


def gelu_parts(pre):
    coeff = math.sqrt(2.0 / math.pi)
    tangent = jnp.tanh(coeff * (pre + 0.044715 * pre * pre * pre))
    activated = 0.5 * pre * (1.0 + tangent)
    slope = 0.5 * (1.0 + tangent) + 0.5 * pre * (1.0 - tangent * tangent) * coeff * (
        1.0 + 3.0 * 0.044715 * pre * pre
    )
    return (activated, slope)


def after(v, *done):
    return lax.optimization_barrier((v, done))[0]


def ordered(even, ours, other, axis):
    return jnp.where(
        even, jnp.concatenate([ours, other], axis), jnp.concatenate([other, ours], axis)
    )


def halves(v, even):
    n = v.shape[-1] // 2
    left, right = v[..., :n], v[..., n:]
    return jnp.where(even, left, right), jnp.where(even, right, left)


def line_send(v, x_core):
    return [lax.ppermute(v, "row", plane_step(shift, x_core)) for shift in SHIFTS]


def line_join(v, pieces, place):
    out = put(jnp.zeros((4,) + v.shape, v.dtype), v, place)
    for shift, piece in zip(SHIFTS, pieces):
        out = put(out, piece, place - shift)
    return out


def line_reduce(v, place, x_core, *done):
    pieces = [
        lax.ppermute(take(v, place + shift), "row", plane_step(shift, x_core)) for shift in SHIFTS
    ]
    total = take(v, place).astype(F32)
    for piece in after(pieces, *done):
        total = total + piece.astype(F32)
    return total


def local(layer_input, out_cotangent, preact, up_weight, down_weight):
    row, z = lax.axis_index("row"), lax.axis_index("col")
    even, x, y = row % 2 == 0, (row // 2) % NX, row // (2 * NX)
    first, second = jnp.where(even, x, y), jnp.where(even, y, x)

    ours, theirs = halves(jnp.stack([out_cotangent, layer_input]), even)
    pair = ordered(even, ours, swap_cores(theirs), 1)
    pieces = line_send(pair, 0)
    cot_line = line_join(pair[0], [p[0] for p in pieces], first)
    input_line = line_join(pair[1], [p[1] for p in pieces], first)

    activated, slope = gelu_parts(after(preact, pair).astype(F32))
    activated = activated.astype(BF16)
    act_below, act_above = send_z(activated, 1), send_z(activated, -1)

    pieces = line_send(cot_line, 1)
    cot = line_join(cot_line, pieces, second)
    cot = jnp.where(even, cot, cot.swapaxes(0, 1)).reshape(-1, cot.shape[-1])
    cot = ordered(even, cot, swap_cores(cot), 1)
    cot = after(cot, act_below, act_above)
    tokens = cot.reshape(NZ, -1, cot.shape[1])
    slope = after(slope, cot_line)

    width = down_weight.shape[0] // CHUNKS
    chunks = range(CHUNKS)

    def share(k, shift):
        return dot(take(tokens, z + shift), down_weight[k * width : (k + 1) * width], 1, 1)

    opposite = [share(k, 2).astype(BF16) for k in chunks]
    far = [send_z_by_core(v) for v in opposite]
    sides = []
    for k in chunks:
        got = far[k].astype(F32)
        zero = jnp.zeros_like(got)
        up = (share(k, 1) + jnp.where(even, got, zero)).astype(BF16)
        down = (share(k, -1) + jnp.where(even, zero, got)).astype(BF16)
        sides.append([send_z(up, 1), send_z(down, -1)])

    own, near = [], []
    for k in chunks:
        if k > 0:
            sides[k] = after(sides[k], own[k - 1])
        total = share(k, 0) + sides[k][0].astype(F32) + sides[k][1].astype(F32)
        own.append((total * slope[:, k * width : (k + 1) * width]).astype(BF16))
        near.append([send_z(own[k], 1), send_z(own[k], -1)])

    input_pieces = line_send(after(input_line, own[-1]), 1)


    last = []
    for k in chunks:
        if k > 0:
            near[k] = after(near[k], onward)
        onward = jnp.where(even, *near[k])
        last.append(send_z_by_core(onward))

    act_far = send_z_by_core(after(jnp.where(even, act_below, act_above), onward))
    act_all = jnp.zeros((NZ,) + activated.shape, BF16)
    for shift, block in ((0, activated), (-1, act_below), (1, act_above), (2, act_far)):
        act_all = put(act_all, block, z + shift)
    down_grad = dot(act_all.reshape(-1, act_all.shape[2]), cot, 0, 0).astype(BF16)

    last[-1] = after(last[-1], input_pieces)
    inputs = line_join(input_line, input_pieces, second)
    inputs = jnp.where(even, inputs, inputs.swapaxes(0, 1)).reshape(-1, inputs.shape[-1])
    inputs = ordered(even, inputs, swap_cores(inputs), 1)

    hidden = jnp.zeros((NZ,) + preact.shape, BF16)
    plane = jnp.zeros((NY,) + (preact.shape[0], up_weight.shape[0] // 2), BF16)
    for shift, blocks in (
        (0, own),
        (-1, [n[0] for n in near]),
        (1, [n[1] for n in near]),
        (2, last),
    ):
        block = jnp.concatenate(blocks, axis=1)
        hidden = put(hidden, block, z + shift)
        ours, theirs = halves(dot(block, up_weight, 1, 1).astype(BF16), even)
        plane = put(plane, (ours + swap_cores(theirs).astype(F32)).astype(BF16), z + shift)
    up_grad = dot(inputs, hidden.reshape(-1, hidden.shape[2]), 0, 0).astype(BF16)

    plane = plane.reshape(NY, NX, -1, plane.shape[-1])
    plane = jnp.where(even, plane, plane.swapaxes(0, 1))
    line = line_reduce(plane, second, 1, up_grad).astype(BF16)
    pair = line_reduce(line, first, 0).astype(BF16)
    n = pair.shape[0] // 2
    upper, lower = pair[:n], pair[n:]
    other = swap_cores(jnp.where(even, lower, upper))
    input_grad = ordered(even, jnp.where(even, upper, lower), other, 1)
    return (input_grad, up_grad, down_grad)


def solution(mesh):
    in_specs = (P("row", "col"), P("row", "col"), P("col", "row"), P("col", "row"), P("row", "col"))
    out_specs = (P("row", "col"), P("col", "row"), P("row", "col"))
    return jax.shard_map(local, mesh=mesh, in_specs=in_specs, out_specs=out_specs, check_vma=False)
```
